32 devices in a mesh: groups: 2 (over y), space: 4 (over z), tm: 2 (over x), head: 2 (over core).
Axes of the slice: x: 2, y: 2, z: 4, core: 2. Of those that a mesh axis runs over, the one named last changes fastest.
Arguments:
- queries: bfloat16 [12288, 3072], P(('groups', 'space', 'tm'), 'head'), parts along dimension 0, may hold values from -40 to 40
- keys: bfloat16 [12288, 3072], P(('groups', 'space', 'tm'), 'head'), parts along dimension 0, may hold values from -12 to 12
- values: bfloat16 [12288, 3072], P(('groups', 'space', 'tm'), 'head'), parts along dimension 0, may hold values from -6 to 6
- text_keys: bfloat16 [128, 3072], P(('groups', 'space'), 'head'), parts along dimension 0, may hold values from -12 to 12
- text_values: bfloat16 [128, 3072], P(('groups', 'space'), 'head'), parts along dimension 0, may hold values from -6 to 6
- face_dest: int32 [512, 2], P(('groups', 'space', 'tm')), parts along dimension 0, may hold values from 0 to 7, all different within a row; in each aligned block of 32 rows (0 to 31, 32 to 63, ...) at most 16 rows name the same one
Outputs:
- attended: bfloat16 [12288, 3072], P(('groups', 'space', 'tm'), 'head'), parts along dimension 0
The draws below stay inside these ranges and needn't reach their ends.
There are 2 independent parts, one for each index of `groups`. The reference program is written for one: setup_inputs(seed, part) draws one part's arguments, and reference() takes and returns one part's arrays. A program takes and returns all parts, laid end to end along the dimension named above; each array names one. Nothing has to cross between parts.
Inputs may be any that keep to these rules, and one draw needn't show every extreme that they name: `face_dest`: each row names 2 different tile groups. Within the 32 rows of one tile group no tile group is named more than 16 times, and in every draw some tile group is named exactly 16 times there.
All inputs are finite; a program needn't handle non-finite values.
Results may differ from the reference program's by a relative error of at most 0.0029.
Values may be sent and summed in bfloat16 or wider, within the bound.
No kernel may reach another device: no remote copies, remote signals or barrier semaphores. Data moves between devices by JAX's collectives and lax.ppermute only.
A program may use at most 64 MiB of HBM per device.

```python
import math
import jax
import jax.numpy as jnp
import numpy as np
from jax import lax

HEADS = 24
HD = 128
TOK_DEV = 768
FBLOCKS = 32
FACE_ROWS = 4
READERS = 2
TILES = 8
SLOTS = 16
TOKENS = 6144
TEXT = 64
FACES = 256
N_SPACE = 4
N_TM = 2


def shared_keys(key):
    base_key = jax.random.fold_in(key, 101)
    return 3.0 * jax.random.truncated_normal(base_key, -4.0, 4.0, (TOKENS, HEADS * HD), jnp.float32)


def draw_keys(key, part):
    drawn = shared_keys(key)
    return drawn.astype(jnp.bfloat16)


def draw_queries(key, part):
    key = jax.random.fold_in(key, 1)
    result = jax.random.truncated_normal(key, -6.0, 6.0, (TOKENS, HEADS * HD), jnp.float32)
    return result.astype(jnp.bfloat16)


def levels(key, dims, pieces, least, largest):
    def one(position, shards_of):
        heights = jax.random.uniform(jax.random.fold_in(jax.random.fold_in(key, 6), position), (shards_of,), jnp.float32, least / len(pieces), largest / len(pieces))
        return jnp.repeat(jnp.exp(heights), dims[position] // shards_of).reshape((-1,) + (1,) * (len(dims) - position - 1))

    factor_of = one(*pieces[0])
    for cut in pieces[1:]:
        factor_of = factor_of * one(*cut)
    return factor_of


def deal_out(own_key, own, number, rows, amount, top, most, slope):
    ranking = jax.random.permutation(own_key, amount)
    packed, usual = load_shares(amount, rows * top, most, slope, True), load_shares(amount, rows * top, most, slope, False)
    places = jnp.arange(amount)

    def named(lengths, offset_by):
        used = int((lengths > 0).sum())
        fixed = max(1, used // 4)
        moved = fixed + (places - fixed + offset_by * (used - fixed)) % max(1, amount - fixed)
        return jnp.zeros((amount,), jnp.int32).at[ranking[jnp.where(places < fixed, places, moved)]].set(jnp.asarray(lengths, jnp.int32))

    lengths = jnp.where(number % 4 == 0, named(packed, number // 4), named(usual, number - number // 4 - 1))
    mixed = jax.random.permutation(jax.random.fold_in(own, 3), amount)
    source_of, sink = mixed[0:amount // 2 * 2:2], mixed[1:amount // 2 * 2:2]
    slack = jnp.minimum(lengths[source_of] - 1, most - lengths[sink]) // 2
    slack = jnp.where((source_of == ranking[0]) | (sink == ranking[0]) | (lengths[sink] == 0), 0, jnp.maximum(slack, 0))
    moved = jax.random.randint(jax.random.fold_in(own, 4), (amount // 2,), 0, 1 << 20) % (slack + 1)
    lengths = lengths.at[source_of].add(-moved).at[sink].add(moved)
    labels = jnp.searchsorted(jnp.cumsum(lengths), jnp.arange(rows * top), side="right").astype(jnp.int32)
    grid = labels.reshape(top, rows).T
    grid = grid[jax.random.permutation(jax.random.fold_in(own, 1), rows)]
    offset_by = jax.random.randint(jax.random.fold_in(own, 2), (rows, 1), 0, top)
    return jnp.take_along_axis(grid, (jnp.arange(top)[None, :] + offset_by) % top, axis=1)


def load_shares(count, total, reach, lean, full):
    portions = [(1 << 20) // math.isqrt(standing ** lean) + 1 for standing in range(1, count + 1)]
    largest = reach if full else min(reach, max(-(-total // count), total * portions[0] // sum(portions)))
    least = 1 if total - largest >= count - 1 else 0
    counts, surplus = [largest] + [least] * (count - 1), total - largest - least * (count - 1)
    while surplus > 0:
        free = [i for i in range(1, count) if counts[i] < largest] or [i for i in range(1, count) if counts[i] < reach]
        mass, left = sum([portions[i] for i in free]), surplus
        for i in free:
            extra = min(reach - counts[i], max(1, left * portions[i] // mass), surplus)
            counts[i] = counts[i] + extra
            surplus = surplus - extra
    return np.array(counts)


def centred(own_key, dims, deviation, reach, shards=(), kind=jnp.bfloat16):
    factor_of = levels(own_key, dims, shards, -0.22, 0.18) if shards else 1.0
    array = jax.random.normal(own_key, dims, jnp.float32) * deviation * factor_of
    return jnp.minimum(jnp.maximum(array, -reach), reach).astype(kind)


def setup_inputs(seed: int = 0, part: int = 0) -> dict:
    arg_keys = jax.random.split(jax.random.key(seed), 7)
    part_splits = jax.random.split(jax.random.fold_in(arg_keys[6], part), 7)
    queries = draw_queries(jax.random.fold_in(jax.random.fold_in(arg_keys[6], part), 71), part)
    keys = draw_keys(jax.random.fold_in(jax.random.fold_in(arg_keys[6], part), 71), part)
    values = centred(part_splits[2], (TOKENS, HEADS * HD), 1.0, 6.0, ((0, 8), (1, 2)))
    text_keys = centred(part_splits[3], (TEXT, HEADS * HD), 3.0, 12.0, ((0, 4), (1, 2)))
    text_values = centred(part_splits[4], (TEXT, HEADS * HD), 1.0, 6.0, ((0, 4), (1, 2)))
    face_dest_keys = jax.random.split(jax.random.fold_in(part_splits[5], 1), FACES // FBLOCKS)
    face_dest_turns = jax.random.permutation(jax.random.fold_in(part_splits[5], 3), FACES // FBLOCKS)
    face_dest = jax.vmap(lambda own, number: deal_out(jax.random.fold_in(part_splits[5], 2), own, number, FBLOCKS, TILES, READERS, SLOTS, 2))(face_dest_keys, face_dest_turns).reshape((FACES, READERS))
    return {"queries": queries, "keys": keys, "values": values, "text_keys": text_keys, "text_values": text_values, "face_dest": face_dest}


def face_selection(face_dest, tile_count, slot_count):
    window_blocks, readers = face_dest.shape
    flat_dest = face_dest.reshape(-1)
    owners = jnp.arange(tile_count, dtype=jnp.int32)
    matches = (flat_dest[:, None] == owners[None, :]).astype(jnp.int32)
    earlier = jnp.cumsum(matches, axis=0) - matches
    slot_rank = lax.optimization_barrier(jnp.sum(earlier * matches, axis=1))
    target = flat_dest * slot_count + slot_rank
    places = jnp.arange(tile_count * slot_count, dtype=jnp.int32)
    chosen = (places[:, None] == target[None, :]).astype(jnp.float32)
    return lax.optimization_barrier(jnp.sum(chosen.reshape(tile_count * slot_count, window_blocks, readers), axis=2))

def reference(queries, keys, values, text_keys, text_values, face_dest):
    tile_count = N_SPACE * N_TM
    feature_width = HEADS * HD
    face_span = FBLOCKS * FACE_ROWS
    score_scale = 1.0 / math.sqrt(HD)
    grouped_destination = face_dest.reshape(tile_count, FBLOCKS, READERS)

    def select_one(group_dest):
        return face_selection(group_dest, tile_count, SLOTS)
    chosen = jax.vmap(select_one)(grouped_destination).reshape(tile_count, tile_count, SLOTS, FBLOCKS)
    tile_queries = queries.reshape(tile_count, TOK_DEV, feature_width)
    tile_keys = keys.reshape(tile_count, TOK_DEV, feature_width)
    per_tile_values = values.reshape(tile_count, TOK_DEV, feature_width)
    window_face_keys = tile_keys[:, :face_span].reshape(tile_count, FBLOCKS, FACE_ROWS * feature_width).astype(jnp.float32)
    window_face_values = per_tile_values[:, :face_span].reshape(tile_count, FBLOCKS, FACE_ROWS * feature_width).astype(jnp.float32)
    text_key_rows = text_keys.astype(jnp.float32)
    text_value_rows = text_values.astype(jnp.float32)

    def one_tile(tile_index):
        selection_index = chosen[:, tile_index]
        gathered_keys = jnp.einsum('lur,lrz->luz', selection_index, window_face_keys, precision=lax.Precision.HIGHEST)
        gathered_values = jnp.einsum('lur,lrz->luz', selection_index, window_face_values, precision=lax.Precision.HIGHEST)
        live_slots = lax.optimization_barrier(jnp.sum(selection_index, axis=2)).reshape(-1)
        live_rows = jnp.repeat(live_slots, FACE_ROWS) > 0.5
        all_keys = jnp.concatenate([tile_keys[tile_index].astype(jnp.float32), gathered_keys.reshape(-1, feature_width), text_key_rows], axis=0)
        all_values = jnp.concatenate([per_tile_values[tile_index].astype(jnp.float32), gathered_values.reshape(-1, feature_width), text_value_rows], axis=0)
        key_mask = jnp.concatenate([jnp.ones((TOK_DEV,), bool), live_rows, jnp.ones((TEXT,), bool)])
        query_rows = tile_queries[tile_index].astype(jnp.float32).reshape(TOK_DEV, HEADS, HD)
        key_heads = all_keys.reshape(-1, HEADS, HD)
        value_heads = all_values.reshape(-1, HEADS, HD)
        scores = jnp.einsum('rhd,khd->hrk', query_rows, key_heads, precision=lax.Precision.HIGHEST) * score_scale
        scores = jnp.where(key_mask[None, None, :], scores, -jnp.inf)
        score_top = lax.optimization_barrier(jnp.max(scores, axis=2, keepdims=True))
        probs = jnp.exp(scores - score_top)
        totals = lax.optimization_barrier(jnp.sum(probs, axis=2, keepdims=True))
        weights = probs.astype(jnp.bfloat16).astype(jnp.float32)
        mixed = jnp.einsum('hrk,khd->hrd', weights, value_heads, precision=lax.Precision.HIGHEST) / totals
        return jnp.transpose(mixed, (1, 0, 2)).reshape(TOK_DEV, feature_width).astype(jnp.bfloat16)
    result = lax.map(one_tile, jnp.arange(tile_count, dtype=jnp.int32))
    return result.reshape(TOKENS, feature_width)
```

```python
import functools
import math

import jax
import jax.numpy as jnp
from jax import lax
from jax.experimental import pallas as pl
from jax.experimental.pallas import tpu as pltpu
from jax.sharding import PartitionSpec as P

HD = 128
FACE_ROWS = 4
GROUPS = 3
TILE_Q = 256
LOG2E = 1.4426950408889634
BF = jnp.bfloat16
F32 = jnp.float32


def face_selection(face_dest, tile_count, slot_count):
    window_blocks, readers = face_dest.shape
    flat_dest = face_dest.reshape(-1)
    owners = jnp.arange(tile_count, dtype=jnp.int32)
    matches = (flat_dest[:, None] == owners[None, :]).astype(jnp.int32)
    earlier = jnp.cumsum(matches, axis=0) - matches
    slot_rank = jnp.sum(earlier * matches, axis=1)
    target = flat_dest * slot_count + slot_rank
    places = jnp.arange(tile_count * slot_count, dtype=jnp.int32)
    chosen = (places[:, None] == target[None, :]).astype(jnp.float32)
    return jnp.sum(chosen.reshape(tile_count * slot_count, window_blocks, readers), axis=2)


def attention_kernel(has_out, part_count, *refs):
    q_ref, k_ref, v_ref, text_k_ref, text_v_ref, live_ref = refs[:6]
    part_refs = refs[6 : 6 + part_count]
    out_ref, key_rows, value_rows = refs[6 + part_count + has_out :]
    tok_rows = k_ref.shape[0]
    text_rows = text_k_ref.shape[0]
    received = live_ref.shape[0]
    scale = LOG2E / math.sqrt(HD)
    key_rows[0:tok_rows, :] = k_ref[...]
    value_rows[0:tok_rows, 0:HD] = v_ref[...]
    value_rows[0:tok_rows, HD:] = jnp.ones((tok_rows, HD), BF)
    at = tok_rows
    spare = k_ref[0:1, :]
    for part in part_refs:
        half = part.shape[0] // 2
        flags = live_ref[at - tok_rows : at - tok_rows + half, :]
        key_rows[at : at + half, :] = jnp.where(flags > 0, part[0:half, :], spare)
        value_rows[at : at + half, 0:HD] = part[half:, :]
        value_rows[at : at + half, HD:] = flags
        at += half
    key_rows[at:, :] = text_k_ref[...]
    value_rows[at:, 0:HD] = text_v_ref[...]
    value_rows[at:, HD:] = jnp.ones((text_rows, HD), BF)
    for start in range(0, q_ref.shape[0], TILE_Q):
        scores = lax.dot_general(
            q_ref[start : start + TILE_Q, :],
            key_rows[...],
            (((1,), (1,)), ((), ())),
            preferred_element_type=F32,
        )
        top = jnp.max(scores, axis=1, keepdims=True)
        weights = jnp.exp2((scores - top) * scale).astype(BF)
        mixed = jnp.dot(weights, value_rows[...], preferred_element_type=F32)
        out_ref[start : start + TILE_Q, :] = (mixed[:, :HD] / mixed[:, HD:]).astype(BF)


def attention(group, heads, queries, keys, values, text_k, text_v, live, parts, out):
    tok_rows, width = queries.shape
    text_rows = text_k.shape[0]
    received = live.shape[0]
    total = tok_rows + received + text_rows
    first = group * heads
    col = lambda h: (0, first + h)
    here = lambda h: (0, h)
    specs = [
        pl.BlockSpec((tok_rows, HD), col),
        pl.BlockSpec((tok_rows, HD), col),
        pl.BlockSpec((tok_rows, HD), col),
        pl.BlockSpec((text_rows, HD), col),
        pl.BlockSpec((text_rows, HD), col),
        pl.BlockSpec((received, HD), lambda h: (0, 0)),
    ]
    operands = [queries, keys, values, text_k, text_v, live]
    for part in parts:
        specs.append(pl.BlockSpec((part.shape[0], HD), here))
        operands.append(part)
    aliases = {}
    if out is not None:
        aliases = {len(operands): 0}
        specs.append(pl.BlockSpec(memory_space=pl.ANY))
        operands.append(out)
    return pl.pallas_call(
        functools.partial(attention_kernel, int(out is not None), len(parts)),
        grid=(heads,),
        out_shape=jax.ShapeDtypeStruct((tok_rows, width), BF),
        in_specs=specs,
        out_specs=pl.BlockSpec((tok_rows, HD), col),
        scratch_shapes=[pltpu.VMEM((total, HD), BF), pltpu.VMEM((total, 2 * HD), BF)],
        input_output_aliases=aliases,
        compiler_params=pltpu.CompilerParams(vmem_limit_bytes=40 * 1024 * 1024),
        cost_estimate=pl.CostEstimate(
            flops=heads * 6 * HD * tok_rows * total,
            bytes_accessed=heads * HD * 2 * (4 * tok_rows + 2 * received),
            transcendentals=heads * tok_rows * total,
        ),
        name="attention%d" % group,
    )(*operands)


def places_kernel(slot_rows, hits_ref, choose_ref, live_ref):
    span = hits_ref.shape[1]
    sources = 4
    hits = hits_ref[...]
    row = lax.broadcasted_iota(jnp.int32, (span, span), 0)
    column = lax.broadcasted_iota(jnp.int32, (span, span), 1)
    before = (row < column) & (row % FACE_ROWS == column % FACE_ROWS)
    rank = jnp.dot(hits.astype(BF), before.astype(BF), preferred_element_type=F32)
    member = (lax.broadcasted_iota(jnp.int32, hits.shape, 1) % FACE_ROWS).astype(F32)
    target = jnp.where(hits > 0, rank * FACE_ROWS + member, -1.0)
    slot = lax.broadcasted_iota(jnp.int32, (slot_rows, span), 0).astype(F32)
    ones = jnp.ones((span, HD), BF)
    for source in range(sources):
        mine = (slot == target[source : source + 1, :]).astype(F32).astype(BF)
        sent = (slot == target[sources + source : sources + source + 1, :]).astype(F32).astype(BF)
        come = (slot == target[2 * sources + source : 2 * sources + source + 1, :]).astype(F32).astype(BF)
        base = source * slot_rows
        choose_ref[2 * base : 2 * base + slot_rows, :] = mine
        choose_ref[2 * base + slot_rows : 2 * base + 2 * slot_rows, :] = sent
        live_ref[base : base + slot_rows, :] = jnp.dot(mine, ones, preferred_element_type=F32).astype(BF)
        base += sources * slot_rows
        live_ref[base : base + slot_rows, :] = jnp.dot(come, ones, preferred_element_type=F32).astype(BF)


def pick_kernel(slot_rows, choose_ref, own_ref, pair_ref, pa_ref, pb_ref, qa_ref, qb_ref, mine_ref, sent_ref):
    half = own_ref.shape[0] // 2
    block = 4 * slot_rows
    for source in range(4):
        choose = choose_ref[2 * slot_rows * source : 2 * slot_rows * (source + 1), :]
        for part in range(2):
            rows = slice(part * half, (part + 1) * half)
            if source == 0:
                held = own_ref[rows, :]
            elif source == 1:
                held = pair_ref[rows, :]
            elif source == 2:
                held = pa_ref[rows, :] + qa_ref[rows, :]
            else:
                held = pb_ref[rows, :] + qb_ref[rows, :]
            got = jnp.dot(choose, held, preferred_element_type=F32).astype(BF)
            base = part * block + source * slot_rows
            mine_ref[base : base + slot_rows, :] = got[:slot_rows, :]
            sent_ref[base : base + slot_rows, :] = got[slot_rows:, :]


def pick(group, slot_rows, choose, arrays):
    span2, width = arrays[0].shape
    whole = lambda a: pl.BlockSpec(a.shape, lambda: (0, 0))
    shape = jax.ShapeDtypeStruct((8 * slot_rows, width), BF)
    spec = pl.BlockSpec(shape.shape, lambda: (0, 0))
    return pl.pallas_call(
        functools.partial(pick_kernel, slot_rows),
        out_shape=(shape, shape),
        in_specs=[whole(a) for a in (choose, *arrays)],
        out_specs=(spec, spec),
        compiler_params=pltpu.CompilerParams(vmem_limit_bytes=24 * 1024 * 1024),
        cost_estimate=pl.CostEstimate(
            flops=4 * 2 * 2 * 2 * slot_rows * span2 // 2 * width,
            bytes_accessed=8 * span2 * width * 2,
            transcendentals=0,
        ),
        name="pick%d" % group,
    )(choose, *arrays)


def chained(queries, keys, values, text_keys, text_values, face_dest):
    spaces = lax.axis_size("space")
    frames = lax.axis_size("tm")
    tile_count = spaces * frames
    window_blocks, readers = face_dest.shape
    tok_rows, width = keys.shape
    slot_count = max(2, 2 * window_blocks * readers // tile_count)
    span = window_blocks * FACE_ROWS
    slot_rows = slot_count * FACE_ROWS
    z = lax.axis_index("space")
    x = lax.axis_index("tm")
    head_count = width // HD
    heads = head_count // GROUPS
    cols = heads * HD

    ends = [(0, 1), (1, 0), (2, 3), (3, 2)]
    inner = [(1, 2), (2, 1)]
    outward = [(1, 0), (2, 3)]
    own = [
        jnp.concatenate(
            [keys[:span, g * cols : (g + 1) * cols], values[:span, g * cols : (g + 1) * cols]], axis=0
        )
        for g in range(GROUPS)
    ]
    all_dest = lax.all_gather(face_dest, ("space", "tm"), axis=0, tiled=False)
    text = lax.all_gather(jnp.stack([text_keys, text_values]), "space", axis=1, tiled=True)
    all_dest = all_dest.reshape(spaces, frames, window_blocks, readers)
    order = jnp.where(z < 2, jnp.array([0, 1, 2, 3]), jnp.array([3, 2, 1, 0]))
    swap = (z == 1) | (z == 2)
    order = jnp.where(swap, jnp.stack([order[1], order[0], order[2], order[3]]), order)
    dest = all_dest[order]
    mine_line = lax.dynamic_index_in_dim(dest, x, 1, keepdims=False)
    other_line = lax.dynamic_index_in_dim(dest, 1 - x, 1, keepdims=False)
    me = z * frames + x
    partner = z * frames + 1 - x
    hits = jnp.stack(
        [
            jnp.any(mine_line == me, axis=2),
            jnp.any(mine_line == partner, axis=2),
            jnp.any(other_line == me, axis=2),
            jnp.zeros((spaces, window_blocks), bool),
        ]
    ).astype(F32)
    hits = jnp.repeat(hits.reshape(4 * spaces, window_blocks), FACE_ROWS, axis=1)
    choose, live = pl.pallas_call(
        functools.partial(places_kernel, slot_rows),
        out_shape=(
            jax.ShapeDtypeStruct((8 * slot_rows, span), BF),
            jax.ShapeDtypeStruct((8 * slot_rows, HD), BF),
        ),
        name="places",
    )(hits)

    pair = [lax.ppermute(a, "space", ends) for a in own]
    pa = [lax.ppermute(a, "space", inner) for a in own]
    pb = [lax.ppermute(a, "space", inner) for a in pair]
    qa = [lax.ppermute(a, "space", outward) for a in pa]
    qb = [lax.ppermute(a, "space", outward) for a in pb]
    out = None
    for g in range(GROUPS):
        mine, sent = pick(g, slot_rows, choose, (own[g], pair[g], pa[g], pb[g], qa[g], qb[g]))
        came = lax.ppermute(sent, "tm", [(0, 1), (1, 0)])
        out = attention(g, heads, queries, keys, values, text[0], text[1], live, (mine, came), out)
    return out


def exchanged(queries, keys, values, text_keys, text_values, face_dest):
    spaces = lax.axis_size("space")
    frames = lax.axis_size("tm")
    tile_count = spaces * frames
    window_blocks, readers = face_dest.shape
    tok_rows, width = keys.shape
    slot_count = max(2, 2 * window_blocks * readers // tile_count)
    span = window_blocks * FACE_ROWS
    slot_rows = slot_count * FACE_ROWS
    chosen = face_selection(face_dest, tile_count, slot_count)

    def exchange(rows):
        blocks = rows[:span].reshape(window_blocks, FACE_ROWS * width)
        send = jnp.dot(chosen.astype(BF), blocks, preferred_element_type=F32).astype(BF)
        send = send.reshape(tile_count, slot_rows, width)
        got = lax.all_to_all(send, ("space", "tm"), split_axis=0, concat_axis=0, tiled=True)
        return got.reshape(-1, width)

    live_slots = jnp.sum(chosen, axis=1).astype(BF).reshape(tile_count, slot_count)
    got_live = lax.all_to_all(live_slots, ("space", "tm"), split_axis=0, concat_axis=0, tiled=True)
    live = jnp.repeat(got_live.reshape(-1, 1), FACE_ROWS, axis=0)
    live = jnp.broadcast_to(live, (live.shape[0], HD))
    received = jnp.concatenate([exchange(keys), exchange(values)], axis=0)
    text_k = lax.all_gather(text_keys, "space", axis=0, tiled=True)
    text_v = lax.all_gather(text_values, "space", axis=0, tiled=True)
    return attention(0, width // HD, queries, keys, values, text_k, text_v, live, (received,), None)


def on_device(*arrays):
    if lax.axis_size("space") == 4 and lax.axis_size("tm") == 2:
        return chained(*arrays)
    return exchanged(*arrays)


def solution(mesh):
    placed = (
        P(("groups", "space", "tm"), "head"),
        P(("groups", "space", "tm"), "head"),
        P(("groups", "space", "tm"), "head"),
        P(("groups", "space"), "head"),
        P(("groups", "space"), "head"),
        P(("groups", "space", "tm"), None),
    )
    return jax.shard_map(
        on_device,
        mesh=mesh,
        in_specs=placed,
        out_specs=P(("groups", "space", "tm"), "head"),
        check_vma=False,
    )
```

```python
import functools
import math

import jax
import jax.numpy as jnp
from jax import lax
from jax.experimental import pallas as pl
from jax.experimental.pallas import tpu as pltpu
from jax.sharding import PartitionSpec as P

HD = 128
FACE_ROWS = 4
HEAD_CUTS = (6, 6)
STEP_HEADS = 2
TILE_Q = 384
VMEM_BYTES = 60 * 1024 * 1024
LOG2E = 1.4426950408889634
BF = jnp.bfloat16
F32 = jnp.float32


def face_selection(face_dest, tile_count, slot_count):
    window_blocks, readers = face_dest.shape
    flat_dest = face_dest.reshape(-1)
    owners = jnp.arange(tile_count, dtype=jnp.int32)
    matches = (flat_dest[:, None] == owners[None, :]).astype(jnp.int32)
    earlier = jnp.cumsum(matches, axis=0) - matches
    slot_rank = jnp.sum(earlier * matches, axis=1)
    target = flat_dest * slot_count + slot_rank
    places = jnp.arange(tile_count * slot_count, dtype=jnp.int32)
    chosen = (places[:, None] == target[None, :]).astype(jnp.float32)
    return jnp.sum(chosen.reshape(tile_count * slot_count, window_blocks, readers), axis=2)


def attention_kernel(settings, line_ref, *refs):
    tok_rows, slot_rows, text_rows, parts, gathered = settings
    q_ref, k_ref, v_ref = refs[:3]
    arrays = parts // 2 if gathered else parts
    part_refs = refs[3 : 3 + arrays]
    if gathered:
        each = part_refs[0].shape[0] // 2
        part_refs = [part.at[half * each : (half + 1) * each, :] for part in part_refs for half in range(2)]
    mark_refs = refs[3 + arrays : 3 + arrays + parts]
    extra = refs[3 + arrays + parts : -4]
    out_ref, key_rows, value_rows, flag_rows = refs[-4:]
    scale = LOG2E / math.sqrt(HD)
    total = key_rows.shape[1]

    @pl.when(pl.program_id(0) == 0)
    def _():
        for place, mark in enumerate(mark_refs):
            rows = slice(place * slot_rows, (place + 1) * slot_rows)
            if gathered:
                hits = jnp.where(mark[...].astype(F32) == line_ref[1].astype(F32), 1.0, 0.0)
                count = jnp.sum(jnp.max(hits, axis=0, keepdims=True), axis=1, keepdims=True)
                slot = lax.broadcasted_iota(jnp.int32, (slot_rows, HD), 0).astype(F32)
                flag_rows[rows, :] = (slot < count).astype(F32).astype(BF)
            else:
                flag_rows[rows, :] = mark[...]
        for sub in range(STEP_HEADS):
            value_rows[sub, :, HD:] = jnp.ones((total, HD), BF)
            value_rows[sub, tok_rows : tok_rows + parts * slot_rows, HD:] = flag_rows[...]

    for sub in range(STEP_HEADS):
        cols = slice(sub * HD, (sub + 1) * HD)
        key_rows[sub, 0:tok_rows, :] = k_ref[:, cols]
        value_rows[sub, 0:tok_rows, 0:HD] = v_ref[:, cols]
        at = tok_rows
        spare = k_ref[0:1, cols]
        for place, part in enumerate(part_refs):
            flags = flag_rows[place * slot_rows : (place + 1) * slot_rows, :]
            key_rows[sub, at : at + slot_rows, :] = jnp.where(flags > 0, part[0:slot_rows, cols], spare)
            value_rows[sub, at : at + slot_rows, 0:HD] = part[slot_rows : 2 * slot_rows, cols]
            at += slot_rows
        if gathered:
            front = line_ref[0] == 0
            half = parts // 2
            for mine, came in zip(part_refs[:half], part_refs[half:]):
                kept = mine[2 * slot_rows : 2 * slot_rows + text_rows, cols]
                brought = came[2 * slot_rows : 2 * slot_rows + text_rows, cols]
                key_rows[sub, at : at + text_rows, :] = jnp.where(front, kept, brought)
                value_rows[sub, at : at + text_rows, 0:HD] = jnp.where(front, brought, kept)
                at += text_rows
        else:
            key_rows[sub, at:, :] = extra[0][:, cols]
            value_rows[sub, at:, 0:HD] = extra[1][:, cols]
        for start in range(0, tok_rows, TILE_Q):
            rows = slice(start, start + TILE_Q)
            scores = lax.dot_general(
                q_ref[rows, cols], key_rows[sub], (((1,), (1,)), ((), ())), preferred_element_type=F32
            )
            top = jnp.max(scores, axis=1, keepdims=True)
            weights = jnp.exp2((scores - top) * scale).astype(BF)
            mixed = jnp.dot(weights, value_rows[sub], preferred_element_type=F32)
            out_ref[rows, cols] = (mixed[:, :HD] / mixed[:, HD:]).astype(BF)


def attention(first, heads, line, queries, keys, values, parts, marks, text, slot_rows, text_rows, total, out, after):
    tok_rows, width = queries.shape
    wide = STEP_HEADS * HD
    col = lambda h, s: (0, first // STEP_HEADS + h)
    here = lambda h, s: (0, h)
    specs = [pl.BlockSpec((tok_rows, wide), col)] * 3
    operands = [line, queries, keys, values]
    for part in parts:
        specs.append(pl.BlockSpec((part.shape[0], wide), col if part.shape[1] == width else here))
        operands.append(part)
    for mark in marks:
        if text:
            specs.append(pl.BlockSpec((slot_rows, HD), lambda h, s: (0, 0)))
        else:
            for at in (mark.shape[0] // 32 - 1, mark.shape[0] // 16 - 1):
                specs.append(pl.BlockSpec((16, HD), lambda h, s, at=at: (at, 0)))
            operands.append(mark)
        operands.append(mark)
    for words in text:
        specs.append(pl.BlockSpec((words.shape[0], wide), col))
        operands.append(words)
    aliases = {}
    if out is not None:
        aliases = {len(operands): 0}
        specs.append(pl.BlockSpec(memory_space=pl.ANY))
        operands.append(out)
    for array in after:
        specs.append(pl.BlockSpec(memory_space=pl.ANY))
        operands.append(array)
    settings = (tok_rows, slot_rows, text_rows, len(parts) * (1 if text else 2), not text)
    return pl.pallas_call(
        functools.partial(attention_kernel, settings),
        grid_spec=pltpu.PrefetchScalarGridSpec(
            num_scalar_prefetch=1,
            grid=(heads // STEP_HEADS,),
            in_specs=specs,
            out_specs=pl.BlockSpec((tok_rows, wide), col),
            scratch_shapes=[
                pltpu.VMEM((STEP_HEADS, total, HD), BF),
                pltpu.VMEM((STEP_HEADS, total, 2 * HD), BF),
                pltpu.VMEM((settings[3] * slot_rows, HD), BF),
            ],
        ),
        out_shape=jax.ShapeDtypeStruct((tok_rows, width), BF),
        input_output_aliases=aliases,
        compiler_params=pltpu.CompilerParams(vmem_limit_bytes=VMEM_BYTES),
        cost_estimate=pl.CostEstimate(
            flops=heads * HD * tok_rows,
            bytes_accessed=heads * HD * 2 * tok_rows,
            transcendentals=0,
        ),
        name="attention%d" % first,
    )(*operands)


def pick_kernel(slot_rows, span, counts, line_ref, *refs):
    blocks = sum(counts)
    slab_refs, held_refs, (mine_ref, sent_ref) = refs[:blocks], refs[blocks : 2 * blocks], refs[-2:]
    row = lax.broadcasted_iota(jnp.int32, (span, span), 0)
    column = lax.broadcasted_iota(jnp.int32, (span, span), 1)
    before = ((row < column) & (row % FACE_ROWS == column % FACE_ROWS)).astype(F32).astype(BF)
    slot = lax.broadcasted_iota(jnp.int32, (slot_rows, span), 0).astype(F32)
    member = (lax.broadcasted_iota(jnp.int32, (1, span), 1) % FACE_ROWS).astype(F32)
    at = 0
    base = 0
    for count in counts:
        slabs, held = slab_refs[at : at + count], held_refs[at : at + count]
        at += count

        def get(start, rows):
            got = held[0][start : start + rows, :]
            return got if count == 1 else got + held[1][start : start + rows, :]

        dest = slabs[0][...] if count == 1 else slabs[0][...] + slabs[1][...]
        dest = dest.astype(F32)
        rest = held[0].shape[0] - 2 * span
        keys, values = get(0, span), get(span, span)
        for side, target_ref in enumerate((mine_ref, sent_ref)):
            hits = jnp.where(dest == line_ref[1 + side].astype(F32), 1.0, 0.0)
            hits = jnp.max(hits, axis=0, keepdims=True)
            rank = jnp.dot(
                jnp.broadcast_to(hits, (16, span)).astype(BF), before, preferred_element_type=F32
            )[0:1, :]
            target = jnp.where(hits > 0, rank * FACE_ROWS + member, -1.0)
            choose = (slot == target).astype(F32).astype(BF)
            for part, rows in enumerate((keys, values)):
                got = jnp.dot(choose, rows, preferred_element_type=F32).astype(BF)
                here = base + part * slot_rows
                target_ref[here : here + slot_rows, :] = got
            here = base + 2 * slot_rows
            target_ref[here : here + rest, :] = get(2 * span, rest)
        base += 2 * slot_rows + rest


def pick(label, slot_rows, span, line, sources, slabs, after):
    counts = tuple(len(source) for source in sources)
    arrays = [array for source in sources for array in source]
    marks = [array for source in slabs for array in source]
    rows, width = arrays[0].shape
    each = rows - 2 * span + 2 * slot_rows
    shape = jax.ShapeDtypeStruct((each * len(sources), width), BF)
    at = marks[0].shape[0] // 16 - 1
    zero = lambda i, s: (0, 0)
    return pl.pallas_call(
        functools.partial(pick_kernel, slot_rows, span, counts),
        grid_spec=pltpu.PrefetchScalarGridSpec(
            num_scalar_prefetch=1,
            grid=(1,),
            in_specs=[pl.BlockSpec((16, span), lambda i, s: (at, 0))] * len(marks)
            + [pl.BlockSpec(a.shape, zero) for a in arrays]
            + [pl.BlockSpec(memory_space=pl.ANY)] * len(after),
            out_specs=(pl.BlockSpec(shape.shape, zero),) * 2,
        ),
        out_shape=(shape, shape),
        compiler_params=pltpu.CompilerParams(vmem_limit_bytes=VMEM_BYTES),
        cost_estimate=pl.CostEstimate(
            flops=8 * len(sources) * slot_rows * span * width,
            bytes_accessed=6 * len(sources) * span * width * 2,
            transcendentals=0,
        ),
        name="pick_" + label,
    )(line, *marks, *arrays, *after)


def chained(queries, keys, values, text_keys, text_values, face_dest):
    spaces = lax.axis_size("space")
    frames = lax.axis_size("tm")
    tile_count = spaces * frames
    window_blocks, readers = face_dest.shape
    tok_rows, width = keys.shape
    text = text_keys.shape[0]
    slot_count = max(2, 2 * window_blocks * readers // tile_count)
    span = window_blocks * FACE_ROWS
    slot_rows = slot_count * FACE_ROWS
    z = lax.axis_index("space")
    x = lax.axis_index("tm")
    line = jnp.stack([x, z * frames + x, z * frames + 1 - x]).astype(jnp.int32)

    ends = [(0, 1), (1, 0), (2, 3), (3, 2)]
    inner = [(1, 2), (2, 1)]
    outward = [(1, 0), (2, 3)]
    swap = [(0, 1), (1, 0)]
    dest = jnp.repeat(face_dest.T, FACE_ROWS, axis=1)
    dest = jnp.concatenate([dest] * (16 // readers), axis=0).astype(BF)
    words = jnp.where(x == 0, text_keys, text_values)
    slab = jnp.pad(dest, ((0, 0), (0, HEAD_CUTS[0] * HD - span)))
    bundles = []
    column = 0
    for heads in HEAD_CUTS:
        cols = slice(column, column + heads * HD)
        rows = [keys[:span, cols], values[:span, cols], words[:, cols]]
        bundles.append(jnp.concatenate(rows + [slab] if column == 0 else rows, axis=0))
        column += heads * HD
    def take(label, sources, slabs, after):
        kept, sent = pick(label, slot_rows, span, line, sources, slabs, after)
        return kept, lax.ppermute(sent, "tm", swap)

    held, near = [], []
    for g, own in enumerate(bundles):
        pair = lax.ppermute(own, "space", ends)
        pa = lax.ppermute(own, "space", inner)
        if g == 0:
            slabs = ((own,), (pair,))
            near.append(take("near0", slabs, slabs, ()))
        pb = lax.ppermute(pair, "space", inner)
        qa = lax.ppermute(pa, "space", outward)
        if g > 0:
            near.append(take("near%d" % g, ((own,), (pair,)), slabs, (qa,)))
        beyond, _ = lax.optimization_barrier((pb, near[0][0])) if g > 0 else (pb, None)
        qb = lax.ppermute(beyond, "space", outward)
        held.append(((pa, qa), (pb, qb)))
    count = len(HEAD_CUTS)
    far = [take("far%d" % g, held[g], held[0], ()) for g in range(count)]
    out = None
    first = 0
    total = tok_rows + tile_count * slot_rows + spaces * text
    marks = [near[0][0], far[0][0], near[0][1], far[0][1]]
    for g, heads in enumerate(HEAD_CUTS):
        parts = [near[g][0], far[g][0], near[g][1], far[g][1]]
        after = (far[-1][0],) if g == 0 else ()
        out = attention(
            first, heads, line, queries, keys, values, parts, marks, (), slot_rows, text, total, out, after
        )
        first += heads
    return out


def exchanged(queries, keys, values, text_keys, text_values, face_dest):
    spaces = lax.axis_size("space")
    frames = lax.axis_size("tm")
    tile_count = spaces * frames
    window_blocks, readers = face_dest.shape
    tok_rows, width = keys.shape
    slot_count = max(2, 2 * window_blocks * readers // tile_count)
    span = window_blocks * FACE_ROWS
    slot_rows = slot_count * FACE_ROWS
    chosen = face_selection(face_dest, tile_count, slot_count)

    def exchange(rows):
        blocks = rows[:span].reshape(window_blocks, FACE_ROWS * width)
        send = jnp.dot(chosen.astype(BF), blocks, preferred_element_type=F32).astype(BF)
        send = send.reshape(tile_count, slot_rows, width)
        got = lax.all_to_all(send, ("space", "tm"), split_axis=0, concat_axis=0, tiled=True)
        return got.reshape(-1, width)

    live_slots = jnp.sum(chosen, axis=1).astype(BF).reshape(tile_count, slot_count)
    got_live = lax.all_to_all(live_slots, ("space", "tm"), split_axis=0, concat_axis=0, tiled=True)
    live = jnp.repeat(got_live.reshape(-1, 1), FACE_ROWS, axis=0)
    live = jnp.broadcast_to(live, (live.shape[0], HD))
    received = jnp.concatenate([exchange(keys), exchange(values)], axis=0)
    text_k = lax.all_gather(text_keys, "space", axis=0, tiled=True)
    text_v = lax.all_gather(text_values, "space", axis=0, tiled=True)
    rows = live.shape[0]
    total = tok_rows + rows + text_k.shape[0]
    line = lax.axis_index("tm").reshape(1).astype(jnp.int32)
    return attention(
        0, width // HD, line, queries, keys, values, [received], [live], (text_k, text_v), rows, 0, total, None, ()
    )


def on_device(*arrays):
    if lax.axis_size("space") == 4 and lax.axis_size("tm") == 2:
        return chained(*arrays)
    return exchanged(*arrays)


def solution(mesh):
    placed = (
        P(("groups", "space", "tm"), "head"),
        P(("groups", "space", "tm"), "head"),
        P(("groups", "space", "tm"), "head"),
        P(("groups", "space"), "head"),
        P(("groups", "space"), "head"),
        P(("groups", "space", "tm"), None),
    )
    return jax.shard_map(
        on_device,
        mesh=mesh,
        in_specs=placed,
        out_specs=P(("groups", "space", "tm"), "head"),
        check_vma=False,
    )
```

```python
import functools
import math

import jax
import jax.numpy as jnp
from jax import lax
from jax.experimental import pallas as pl
from jax.experimental.pallas import tpu as pltpu
from jax.sharding import PartitionSpec as P

HD = 128
FACE_ROWS = 4
HEAD_CUTS = (6, 6)
STEP_HEADS = 2
TILE_Q = 384
VMEM_BYTES = 60 * 1024 * 1024
LOG2E = 1.4426950408889634
BF = jnp.bfloat16
F32 = jnp.float32


def face_selection(face_dest, tile_count, slot_count):
    window_blocks, readers = face_dest.shape
    flat_dest = face_dest.reshape(-1)
    owners = jnp.arange(tile_count, dtype=jnp.int32)
    matches = (flat_dest[:, None] == owners[None, :]).astype(jnp.int32)
    earlier = jnp.cumsum(matches, axis=0) - matches
    slot_rank = jnp.sum(earlier * matches, axis=1)
    target = flat_dest * slot_count + slot_rank
    places = jnp.arange(tile_count * slot_count, dtype=jnp.int32)
    chosen = (places[:, None] == target[None, :]).astype(jnp.float32)
    return jnp.sum(chosen.reshape(tile_count * slot_count, window_blocks, readers), axis=2)


def tile_kernel(q_ref, k_ref, v_ref, sum_ref, stat_ref, value_rows):
    tok_rows = k_ref.shape[0]
    scale = LOG2E / math.sqrt(HD)

    @pl.when(pl.program_id(0) == 0)
    def _():
        for sub in range(STEP_HEADS):
            value_rows[sub, :, HD:] = jnp.ones((tok_rows, HD), BF)
        stat_ref[...] = jnp.zeros(stat_ref.shape, F32)

    lane = lax.broadcasted_iota(jnp.int32, (TILE_Q, HD), 1)
    for sub in range(STEP_HEADS):
        head = pl.program_id(0) * STEP_HEADS + sub
        cols = slice(sub * HD, (sub + 1) * HD)
        value_rows[sub, :, 0:HD] = v_ref[:, cols]
        for start in range(0, tok_rows, TILE_Q):
            rows = slice(start, start + TILE_Q)
            scores = lax.dot_general(
                q_ref[rows, cols], k_ref[:, cols], (((1,), (1,)), ((), ())), preferred_element_type=F32
            )
            top = jnp.max(scores, axis=1, keepdims=True)
            weights = jnp.exp2((scores - top) * scale).astype(BF)
            mixed = jnp.dot(weights, value_rows[sub], preferred_element_type=F32)
            sum_ref[rows, cols] = mixed[:, :HD]
            kept = jnp.where(lane == head, top, stat_ref[rows, :])
            stat_ref[rows, :] = jnp.where(lane == head + HD // 2, mixed[:, HD:], kept)


def tile_attention(first, heads, queries, keys, values):
    tok_rows, width = queries.shape
    spec = pl.BlockSpec((tok_rows, STEP_HEADS * HD), lambda h: (0, first // STEP_HEADS + h))
    own_spec = pl.BlockSpec((tok_rows, STEP_HEADS * HD), lambda h: (0, h))
    return pl.pallas_call(
        tile_kernel,
        grid=(heads // STEP_HEADS,),
        in_specs=[spec] * 3,
        out_specs=(own_spec, pl.BlockSpec((tok_rows, HD), lambda h: (0, 0))),
        out_shape=(
            jax.ShapeDtypeStruct((tok_rows, heads * HD), F32),
            jax.ShapeDtypeStruct((tok_rows, HD), F32),
        ),
        scratch_shapes=[pltpu.VMEM((STEP_HEADS, tok_rows, 2 * HD), BF)],
        compiler_params=pltpu.CompilerParams(vmem_limit_bytes=VMEM_BYTES),
        cost_estimate=pl.CostEstimate(
            flops=heads * 6 * HD * tok_rows * tok_rows,
            bytes_accessed=heads * HD * 10 * tok_rows,
            transcendentals=heads * tok_rows * tok_rows,
        ),
        name="tile%d" % first,
    )(queries, keys, values)


def attention_kernel(settings, line_ref, *refs):
    slot_rows, text_rows, parts, gathered = settings
    q_ref, k_ref, sum_ref, stat_ref = refs[:4]
    arrays = parts // 2 if gathered else parts
    part_refs = refs[4 : 4 + arrays]
    if gathered:
        each = part_refs[0].shape[0] // 2
        part_refs = [part.at[half * each : (half + 1) * each, :] for part in part_refs for half in range(2)]
    mark_refs = refs[4 + arrays : 4 + arrays + parts]
    extra = refs[4 + arrays + parts : -4]
    out_ref, key_rows, value_rows, flag_rows = refs[-4:]
    scale = LOG2E / math.sqrt(HD)
    total = key_rows.shape[1]

    @pl.when(pl.program_id(0) == 0)
    def _():
        for place, mark in enumerate(mark_refs):
            rows = slice(place * slot_rows, (place + 1) * slot_rows)
            if gathered:
                hits = jnp.where(mark[...].astype(F32) == line_ref[1].astype(F32), 1.0, 0.0)
                count = jnp.sum(jnp.max(hits, axis=0, keepdims=True), axis=1, keepdims=True)
                slot = lax.broadcasted_iota(jnp.int32, (slot_rows, HD), 0).astype(F32)
                flag_rows[rows, :] = (slot < count).astype(F32).astype(BF)
            else:
                flag_rows[rows, :] = mark[...]
        for sub in range(STEP_HEADS):
            value_rows[sub, :, HD:] = jnp.ones((total, HD), BF)
            value_rows[sub, 0 : parts * slot_rows, HD:] = flag_rows[...]

    for sub in range(STEP_HEADS):
        cols = slice(sub * HD, (sub + 1) * HD)
        at = 0
        spare = k_ref[0:1, cols]
        for place, part in enumerate(part_refs):
            flags = flag_rows[place * slot_rows : (place + 1) * slot_rows, :]
            key_rows[sub, at : at + slot_rows, :] = jnp.where(flags > 0, part[0:slot_rows, cols], spare)
            value_rows[sub, at : at + slot_rows, 0:HD] = part[slot_rows : 2 * slot_rows, cols]
            at += slot_rows
        if gathered:
            front = line_ref[0] == 0
            half = parts // 2
            for mine, came in zip(part_refs[:half], part_refs[half:]):
                kept = mine[2 * slot_rows : 2 * slot_rows + text_rows, cols]
                brought = came[2 * slot_rows : 2 * slot_rows + text_rows, cols]
                key_rows[sub, at : at + text_rows, :] = jnp.where(front, kept, brought)
                value_rows[sub, at : at + text_rows, 0:HD] = jnp.where(front, brought, kept)
                at += text_rows
        else:
            key_rows[sub, at:, :] = extra[0][:, cols]
            value_rows[sub, at:, 0:HD] = extra[1][:, cols]
        head = pl.program_id(0) * STEP_HEADS + sub
        lane = lax.broadcasted_iota(jnp.int32, (TILE_Q, HD), 1)
        for start in range(0, q_ref.shape[0], TILE_Q):
            rows = slice(start, start + TILE_Q)
            scores = lax.dot_general(
                q_ref[rows, cols], key_rows[sub], (((1,), (1,)), ((), ())), preferred_element_type=F32
            )
            stats = stat_ref[rows, :]
            tile_top = jnp.sum(jnp.where(lane == head, stats, 0.0), axis=1, keepdims=True)
            tile_total = jnp.sum(jnp.where(lane == head + HD // 2, stats, 0.0), axis=1, keepdims=True)
            top = jnp.maximum(jnp.max(scores, axis=1, keepdims=True), tile_top)
            weights = jnp.exp2((scores - top) * scale).astype(BF)
            mixed = jnp.dot(weights, value_rows[sub], preferred_element_type=F32)
            share = jnp.exp2((tile_top - top) * scale)
            whole = mixed[:, :HD] + share * sum_ref[rows, cols]
            out_ref[rows, cols] = (whole / (mixed[:, HD:] + share * tile_total)).astype(BF)


def attention(first, heads, line, queries, keys, tile, parts, marks, text, slot_rows, text_rows, total, out, after):
    tok_rows, width = queries.shape
    wide = STEP_HEADS * HD
    col = lambda h, s: (0, first // STEP_HEADS + h)
    here = lambda h, s: (0, h)
    specs = [
        pl.BlockSpec((tok_rows, wide), col),
        pl.BlockSpec((16, wide), col),
        pl.BlockSpec((tok_rows, wide), here),
        pl.BlockSpec((tok_rows, HD), lambda h, s: (0, 0)),
    ]
    operands = [line, queries, keys, *tile]
    for part in parts:
        specs.append(pl.BlockSpec((part.shape[0], wide), col if part.shape[1] == width else here))
        operands.append(part)
    for mark in marks:
        if text:
            specs.append(pl.BlockSpec((slot_rows, HD), lambda h, s: (0, 0)))
        else:
            for at in (mark.shape[0] // 32 - 1, mark.shape[0] // 16 - 1):
                specs.append(pl.BlockSpec((16, HD), lambda h, s, at=at: (at, 0)))
            operands.append(mark)
        operands.append(mark)
    for words in text:
        specs.append(pl.BlockSpec((words.shape[0], wide), col))
        operands.append(words)
    aliases = {}
    if out is not None:
        aliases = {len(operands): 0}
        specs.append(pl.BlockSpec(memory_space=pl.ANY))
        operands.append(out)
    for array in after:
        specs.append(pl.BlockSpec(memory_space=pl.ANY))
        operands.append(array)
    settings = (slot_rows, text_rows, len(parts) * (1 if text else 2), not text)
    return pl.pallas_call(
        functools.partial(attention_kernel, settings),
        grid_spec=pltpu.PrefetchScalarGridSpec(
            num_scalar_prefetch=1,
            grid=(heads // STEP_HEADS,),
            in_specs=specs,
            out_specs=pl.BlockSpec((tok_rows, wide), col),
            scratch_shapes=[
                pltpu.VMEM((STEP_HEADS, total, HD), BF),
                pltpu.VMEM((STEP_HEADS, total, 2 * HD), BF),
                pltpu.VMEM((settings[2] * slot_rows, HD), BF),
            ],
        ),
        out_shape=jax.ShapeDtypeStruct((tok_rows, width), BF),
        input_output_aliases=aliases,
        compiler_params=pltpu.CompilerParams(vmem_limit_bytes=VMEM_BYTES),
        cost_estimate=pl.CostEstimate(
            flops=heads * HD * tok_rows,
            bytes_accessed=heads * HD * 2 * tok_rows,
            transcendentals=0,
        ),
        name="attention%d" % first,
    )(*operands)


def pick_kernel(slot_rows, span, counts, line_ref, *refs):
    blocks = sum(counts)
    slab_refs, held_refs, (mine_ref, sent_ref) = refs[:blocks], refs[blocks : 2 * blocks], refs[-2:]
    row = lax.broadcasted_iota(jnp.int32, (span, span), 0)
    column = lax.broadcasted_iota(jnp.int32, (span, span), 1)
    before = ((row < column) & (row % FACE_ROWS == column % FACE_ROWS)).astype(F32).astype(BF)
    slot = lax.broadcasted_iota(jnp.int32, (slot_rows, span), 0).astype(F32)
    member = (lax.broadcasted_iota(jnp.int32, (1, span), 1) % FACE_ROWS).astype(F32)
    at = 0
    base = 0
    for count in counts:
        slabs, held = slab_refs[at : at + count], held_refs[at : at + count]
        at += count

        def get(start, rows):
            got = held[0][start : start + rows, :]
            return got if count == 1 else got + held[1][start : start + rows, :]

        dest = slabs[0][...] if count == 1 else slabs[0][...] + slabs[1][...]
        dest = dest.astype(F32)
        rest = held[0].shape[0] - 2 * span
        keys, values = get(0, span), get(span, span)
        for side, target_ref in enumerate((mine_ref, sent_ref)):
            hits = jnp.where(dest == line_ref[1 + side].astype(F32), 1.0, 0.0)
            hits = jnp.max(hits, axis=0, keepdims=True)
            rank = jnp.dot(
                jnp.broadcast_to(hits, (16, span)).astype(BF), before, preferred_element_type=F32
            )[0:1, :]
            target = jnp.where(hits > 0, rank * FACE_ROWS + member, -1.0)
            choose = (slot == target).astype(F32).astype(BF)
            for part, rows in enumerate((keys, values)):
                got = jnp.dot(choose, rows, preferred_element_type=F32).astype(BF)
                here = base + part * slot_rows
                target_ref[here : here + slot_rows, :] = got
            here = base + 2 * slot_rows
            target_ref[here : here + rest, :] = get(2 * span, rest)
        base += 2 * slot_rows + rest


def pick(label, slot_rows, span, line, sources, slabs, after):
    counts = tuple(len(source) for source in sources)
    arrays = [array for source in sources for array in source]
    marks = [array for source in slabs for array in source]
    rows, width = arrays[0].shape
    each = rows - 2 * span + 2 * slot_rows
    shape = jax.ShapeDtypeStruct((each * len(sources), width), BF)
    at = marks[0].shape[0] // 16 - 1
    zero = lambda i, s: (0, 0)
    return pl.pallas_call(
        functools.partial(pick_kernel, slot_rows, span, counts),
        grid_spec=pltpu.PrefetchScalarGridSpec(
            num_scalar_prefetch=1,
            grid=(1,),
            in_specs=[pl.BlockSpec((16, span), lambda i, s: (at, 0))] * len(marks)
            + [pl.BlockSpec(a.shape, zero) for a in arrays]
            + [pl.BlockSpec(memory_space=pl.ANY)] * len(after),
            out_specs=(pl.BlockSpec(shape.shape, zero),) * 2,
        ),
        out_shape=(shape, shape),
        compiler_params=pltpu.CompilerParams(vmem_limit_bytes=VMEM_BYTES),
        cost_estimate=pl.CostEstimate(
            flops=8 * len(sources) * slot_rows * span * width,
            bytes_accessed=6 * len(sources) * span * width * 2,
            transcendentals=0,
        ),
        name="pick_" + label,
    )(line, *marks, *arrays, *after)


def chained(queries, keys, values, text_keys, text_values, face_dest):
    spaces = lax.axis_size("space")
    frames = lax.axis_size("tm")
    tile_count = spaces * frames
    window_blocks, readers = face_dest.shape
    tok_rows, width = keys.shape
    text = text_keys.shape[0]
    slot_count = max(2, 2 * window_blocks * readers // tile_count)
    span = window_blocks * FACE_ROWS
    slot_rows = slot_count * FACE_ROWS
    z = lax.axis_index("space")
    x = lax.axis_index("tm")
    line = jnp.stack([x, z * frames + x, z * frames + 1 - x]).astype(jnp.int32)

    ends = [(0, 1), (1, 0), (2, 3), (3, 2)]
    inner = [(1, 2), (2, 1)]
    outward = [(1, 0), (2, 3)]
    swap = [(0, 1), (1, 0)]
    dest = jnp.repeat(face_dest.T, FACE_ROWS, axis=1)
    dest = jnp.concatenate([dest] * (16 // readers), axis=0).astype(BF)
    words = jnp.where(x == 0, text_keys, text_values)
    slab = jnp.pad(dest, ((0, 0), (0, HEAD_CUTS[0] * HD - span)))
    bundles = []
    column = 0
    for heads in HEAD_CUTS:
        cols = slice(column, column + heads * HD)
        rows = [keys[:span, cols], values[:span, cols], words[:, cols]]
        bundles.append(jnp.concatenate(rows + [slab] if column == 0 else rows, axis=0))
        column += heads * HD
    tiles = []
    for heads in HEAD_CUTS:
        tiles.append(tile_attention(len(tiles) * heads, heads, queries, keys, values))
    def take(label, sources, slabs, after):
        kept, sent = pick(label, slot_rows, span, line, sources, slabs, after)
        return kept, lax.ppermute(sent, "tm", swap)

    held, near = [], []
    for g, own in enumerate(bundles):
        pair = lax.ppermute(own, "space", ends)
        pa = lax.ppermute(own, "space", inner)
        if g == 0:
            slabs = ((own,), (pair,))
            near.append(take("near0", slabs, slabs, ()))
        pair, _ = lax.optimization_barrier((pair, tiles[g][1]))
        pb = lax.ppermute(pair, "space", inner)
        qa = lax.ppermute(pa, "space", outward)
        if g > 0:
            near.append(take("near%d" % g, ((own,), (pair,)), slabs, (qa,)))
        beyond, _ = lax.optimization_barrier((pb, near[0][0])) if g > 0 else (pb, None)
        qb = lax.ppermute(beyond, "space", outward)
        held.append(((pa, qa), (pb, qb)))
    count = len(HEAD_CUTS)
    far = [take("far%d" % g, held[g], held[0], ()) for g in range(count)]
    out = None
    first = 0
    total = tile_count * slot_rows + spaces * text
    marks = [near[0][0], far[0][0], near[0][1], far[0][1]]
    for g, heads in enumerate(HEAD_CUTS):
        parts = [near[g][0], far[g][0], near[g][1], far[g][1]]
        after = (far[-1][0],) if g == 0 else ()
        out = attention(
            first, heads, line, queries, keys, tiles[g], parts, marks, (), slot_rows, text, total, out, after
        )
        first += heads
    return out


def exchanged(queries, keys, values, text_keys, text_values, face_dest):
    spaces = lax.axis_size("space")
    frames = lax.axis_size("tm")
    tile_count = spaces * frames
    window_blocks, readers = face_dest.shape
    tok_rows, width = keys.shape
    slot_count = max(2, 2 * window_blocks * readers // tile_count)
    span = window_blocks * FACE_ROWS
    slot_rows = slot_count * FACE_ROWS
    chosen = face_selection(face_dest, tile_count, slot_count)

    def exchange(rows):
        blocks = rows[:span].reshape(window_blocks, FACE_ROWS * width)
        send = jnp.dot(chosen.astype(BF), blocks, preferred_element_type=F32).astype(BF)
        send = send.reshape(tile_count, slot_rows, width)
        got = lax.all_to_all(send, ("space", "tm"), split_axis=0, concat_axis=0, tiled=True)
        return got.reshape(-1, width)

    live_slots = jnp.sum(chosen, axis=1).astype(BF).reshape(tile_count, slot_count)
    got_live = lax.all_to_all(live_slots, ("space", "tm"), split_axis=0, concat_axis=0, tiled=True)
    live = jnp.repeat(got_live.reshape(-1, 1), FACE_ROWS, axis=0)
    live = jnp.broadcast_to(live, (live.shape[0], HD))
    received = jnp.concatenate([exchange(keys), exchange(values)], axis=0)
    text_k = lax.all_gather(text_keys, "space", axis=0, tiled=True)
    text_v = lax.all_gather(text_values, "space", axis=0, tiled=True)
    rows = live.shape[0]
    total = rows + text_k.shape[0]
    line = lax.axis_index("tm").reshape(1).astype(jnp.int32)
    tile = tile_attention(0, width // HD, queries, keys, values)
    return attention(
        0, width // HD, line, queries, keys, tile, [received], [live], (text_k, text_v), rows, 0, total, None, ()
    )


def on_device(*arrays):
    if lax.axis_size("space") == 4 and lax.axis_size("tm") == 2:
        return chained(*arrays)
    return exchanged(*arrays)


def solution(mesh):
    placed = (
        P(("groups", "space", "tm"), "head"),
        P(("groups", "space", "tm"), "head"),
        P(("groups", "space", "tm"), "head"),
        P(("groups", "space"), "head"),
        P(("groups", "space"), "head"),
        P(("groups", "space", "tm"), None),
    )
    return jax.shard_map(
        on_device,
        mesh=mesh,
        in_specs=placed,
        out_specs=P(("groups", "space", "tm"), "head"),
        check_vma=False,
    )
```
